32 devices in a mesh: head: 2 (over core), vis: 16 (over z, y, x).
Axes of the slice: x: 2, y: 2, z: 4, core: 2. Of those that a mesh axis runs over, the one named last changes fastest.
Arguments:
- queries: bfloat16 [2, 128, 4096], P(None, 'vis', 'head'), may hold values from -24 to 24
- keys: bfloat16 [2, 6400, 1024], P(None, 'vis', 'head'), may hold values from -24 to 24
- values: bfloat16 [2, 6400, 1024], P(None, 'vis', 'head'), may hold values from -6 to 6
- d_out: bfloat16 [2, 128, 4096], P(None, 'vis', 'head'), may hold values from -6 to 6
- q_weight: bfloat16 [4096, 4096], P('vis', 'head'), may hold values from -0.09375 to 0.09375
Outputs:
- d_input: bfloat16 [2, 128, 4096], P(None, 'head', 'vis')
- d_keys: bfloat16 [2, 6400, 1024], P(None, 'vis', 'head')
- d_values: bfloat16 [2, 6400, 1024], P(None, 'vis', 'head')
The draws below stay inside these ranges and needn't reach their ends.
All inputs are finite; a program needn't handle non-finite values.
Results may differ from the reference program's by a relative error of at most 0.014.
Values may be sent and summed in bfloat16 or wider, within the bound.
A program may use at most 64 MiB of HBM per device.

```python
import jax
import jax.numpy as jnp
from jax import lax

D = 4096
HQ = 32
KVH = 8
HD = 128
BATCH = 2
TEXT = 128
VIS = 6400


def draw_queries(key, part):
    width = HQ * HD
    drawn = jnp.clip(jax.random.normal(jax.random.fold_in(key, 11), (BATCH, TEXT, width), jnp.float32), -6.0, 6.0)
    return drawn.astype(jnp.bfloat16)


def draw_keys(key, part):
    width = KVH * HD
    drawn = jnp.clip(jax.random.normal(jax.random.fold_in(key, 23), (BATCH, VIS, width), jnp.float32), -6.0, 6.0)
    return drawn.astype(jnp.bfloat16)


def levels(stream_key, dims, pieces, smallest, largest):
    def one(dim, parts):
        heights = jax.random.uniform(jax.random.fold_in(jax.random.fold_in(stream_key, 6), dim), (parts,), jnp.float32, smallest / len(pieces), largest / len(pieces))
        return jnp.repeat(jnp.exp(heights), dims[dim] // parts).reshape((-1,) + (1,) * (len(dims) - dim - 1))

    gain = one(*pieces[0])
    for cut in pieces[1:]:
        gain = gain * one(*cut)
    return gain


def noise(stream_key, dims, deviation, bound, pieces=(), dtype=jnp.bfloat16):
    values = jax.random.normal(stream_key, dims, jnp.float32) * deviation
    if len(pieces) > 0:
        values = levels(stream_key, dims, pieces, -0.22, 0.18) * values
    return jnp.clip(values, min=-bound, max=bound).astype(dtype)


def setup_inputs(seed: int = 0) -> dict:
    seeds = jax.random.split(jax.random.key(seed), 6)
    queries = draw_queries(jax.random.fold_in(seeds[5], 71), 0)
    keys = draw_keys(jax.random.fold_in(seeds[5], 71), 0)
    values = noise(seeds[2], (BATCH, VIS, KVH * HD), 1.0, 6.0, ((1, 16), (2, 2)))
    d_out = noise(seeds[3], (BATCH, TEXT, HQ * HD), 1.0, 6.0, ((1, 16), (2, 2)))
    q_weight = noise(seeds[4], (D, HQ * HD), (HQ * HD) ** -0.5, 0.09375, ((0, 16), (1, 2)))
    return dict(queries=queries, keys=keys, values=values, d_out=d_out, q_weight=q_weight)


def group_backward(operands):
    query_group, grad_group, key_group, value_group = operands
    inv_root = HD ** -0.5
    query_full = query_group.astype(jnp.float32)
    grad_full = grad_group.astype(jnp.float32)
    key_full = key_group.astype(jnp.float32)
    value_full = value_group.astype(jnp.float32)
    scores = jnp.einsum("btgd,bjd->bgtj", query_full, key_full) * inv_root
    log_total = jax.nn.logsumexp(scores, axis=-1, keepdims=True)
    probs = jnp.exp(scores - log_total)
    probs_low = lax.optimization_barrier(probs.astype(jnp.bfloat16)).astype(jnp.float32)
    grad_probs = jnp.einsum("btgd,bjd->bgtj", grad_full, value_full)
    delta_sum = jnp.sum(probs * grad_probs, axis=-1, keepdims=True)
    grad_scores = probs * (grad_probs - delta_sum)
    grad_low = lax.optimization_barrier(grad_scores.astype(jnp.bfloat16)).astype(jnp.float32)
    grad_query = (jnp.einsum("bgtj,bjd->btgd", grad_low, key_full) * inv_root).astype(jnp.bfloat16)
    grad_key = (jnp.einsum("bgtj,btgd->bjd", grad_low, query_full) * inv_root).astype(jnp.bfloat16)
    grad_value = jnp.einsum("bgtj,btgd->bjd", probs_low, grad_full).astype(jnp.bfloat16)
    return grad_query, grad_key, grad_value


def reference(queries, keys, values, d_out, q_weight):
    groups = HQ // KVH
    batch_size, text_len, _ = queries.shape
    vis_len = keys.shape[1]
    query_heads = jnp.moveaxis(queries.reshape(batch_size, text_len, KVH, groups, HD), 2, 0)
    grad_heads = jnp.moveaxis(d_out.reshape(batch_size, text_len, KVH, groups, HD), 2, 0)
    key_heads = jnp.moveaxis(keys.reshape(batch_size, vis_len, KVH, HD), 2, 0)
    value_heads = jnp.moveaxis(values.reshape(batch_size, vis_len, KVH, HD), 2, 0)
    grad_query, grad_key, grad_value = lax.map(group_backward, (query_heads, grad_heads, key_heads, value_heads))
    grad_query = jnp.moveaxis(grad_query, 0, 2).reshape(batch_size, text_len, KVH * groups * HD)
    d_keys = jnp.moveaxis(grad_key, 0, 2).reshape(batch_size, vis_len, KVH * HD)
    d_values = jnp.moveaxis(grad_value, 0, 2).reshape(batch_size, vis_len, KVH * HD)
    d_input = jnp.einsum("btq,dq->btd", grad_query.astype(jnp.float32), q_weight.astype(jnp.float32))
    return d_input.astype(jnp.bfloat16), d_keys, d_values
```

```python
import functools
import math

import jax
import jax.numpy as jnp
from jax import lax
from jax.experimental import pallas as pl
from jax.experimental.pallas import tpu as pltpu
from jax.sharding import PartitionSpec as P

HQ = 32
KVH = 8
HD = 128
GROUPS = HQ // KVH
INV_ROOT = HD ** (-0.5)
NT = (((1,), (1,)), ((), ()))
TN = (((0,), (0,)), ((), ()))
NN = (((1,), (0,)), ((), ()))


def dot(x, y, dims):
    return lax.dot_general(x, y, dims, preferred_element_type=jnp.float32)


def kernel(
    outer, inner, heads,
    q_ref, g_ref, k_ref, v_ref, w_ref,
    din_ref, dk_ref, dv_ref,
    gath, probs, gprobs, stat, stat_in, stat_mid, stat_out, scal,
    dq_send, dq_plane, dq_mid, dq_line, gath2, part, part_send, part_in,
    gz_s, gz_r, gp_s, gp_r, sp_s, sp_r, sz_s, sz_r,
    rp_s, rp_r, rz_s, rz_r, hz_s, hz_r, hp_s, hp_r, hd_s, hd_r,
):
    batch, text, width = q_ref.shape
    kv_local = width // (HD * GROUPS)
    chunks = batch * kv_local
    vis = outer * inner
    rows = vis * GROUPS * text
    me = lax.axis_index("vis")
    my_head = lax.axis_index("head")
    line, place = me // inner, lax.rem(me, inner)

    def on_line(step):
        return lax.rem(line + step + outer, outer) * inner + place

    def in_plane(step):
        return line * inner + lax.rem(place + step + inner, inner)

    def other_head(step):
        return lax.rem(my_head + step + heads, heads)

    def copy(src, dst, send, recv, **where):
        return pltpu.make_async_remote_copy(
            src_ref=src, dst_ref=dst, send_sem=send, recv_sem=recv,
            device_id=where, device_id_type=pl.DeviceIdType.MESH,
        )

    barrier = pltpu.get_barrier_semaphore()
    for step in range(1, outer):
        pl.semaphore_signal(barrier, inc=1, device_id={"vis": on_line(step)},
                            device_id_type=pl.DeviceIdType.MESH)
    for step in range(1, inner):
        pl.semaphore_signal(barrier, inc=1, device_id={"vis": in_plane(step)},
                            device_id_type=pl.DeviceIdType.MESH)
    for step in range(1, heads):
        pl.semaphore_signal(barrier, inc=1, device_id={"head": other_head(step)},
                            device_id_type=pl.DeviceIdType.MESH)
    for which, ref in ((0, q_ref), (1, g_ref)):
        for b in range(batch):
            for h in range(kv_local):
                block = [
                    ref[b, :, pl.ds((h * GROUPS + g) * HD, HD)].astype(jnp.float32)
                    for g in range(GROUPS)
                ]
                gath[which, b * kv_local + h, me] = jnp.concatenate(block, 0).astype(jnp.bfloat16)
    pl.semaphore_wait(barrier, outer + inner + heads - 3)

    def gather(slot, line_s, line_r, plane_s, plane_r):
        sent = []

        def spread(step):
            owner = on_line(-step)
            for m in range(1, inner):
                c = copy(slot(owner), slot(owner), plane_s.at[step, m], plane_r.at[step, m],
                         vis=in_plane(m))
                c.start()
                sent.append(c)

        for step in range(1, outer):
            c = copy(slot(me), slot(me), line_s.at[step], line_r.at[step], vis=on_line(step))
            c.start()
            sent.append(c)
        spread(0)
        for step in range(1, outer):
            owner = on_line(-step)
            copy(slot(owner), slot(owner), line_s.at[step], line_r.at[step],
                 vis=on_line(step)).wait_recv()
            spread(step)
        for step in range(outer):
            for m in range(1, inner):
                owner = lax.rem(line - step + outer, outer) * inner + lax.rem(place - m + inner, inner)
                copy(slot(owner), slot(owner), plane_s.at[step, m], plane_r.at[step, m],
                     vis=in_plane(m)).wait_recv()
        return sent

    sent = gather(lambda v: gath.at[:, :, v], gz_s, gz_r, gp_s, gp_r)

    def first(c, _):
        b, h = c // kv_local, lax.rem(c, kv_local)
        lanes = pl.ds(pl.multiple_of(h * HD, HD), HD)
        query = gath[0, c].reshape(rows, HD)
        grad = gath[1, c].reshape(rows, HD)
        scores = dot(k_ref[b, :, lanes], query, NT) * INV_ROOT
        peak = jnp.max(scores, axis=0, keepdims=True)
        weights = jnp.exp(scores - peak)
        grads = dot(v_ref[b, :, lanes], grad, NT)
        probs[c] = weights
        gprobs[c] = grads
        stat[0, pl.ds(c, 1), :] = peak
        stat[1, pl.ds(c, 1), :] = jnp.sum(weights, axis=0, keepdims=True)
        stat[2, pl.ds(c, 1), :] = jnp.sum(weights * grads, axis=0, keepdims=True)
        return 0

    lax.fori_loop(0, chunks, first, 0)

    def combine(parts):
        peak = functools.reduce(jnp.maximum, [p[0] for p in parts])
        scale = [jnp.exp(p[0] - peak) for p in parts]
        total = sum(p[1] * s for p, s in zip(parts, scale))
        weighted = sum(p[2] * s for p, s in zip(parts, scale))
        return peak, total, weighted

    for m in range(1, inner):
        c = copy(stat, stat_in.at[m], sp_s.at[m], sp_r.at[m], vis=in_plane(m))
        c.start()
        sent.append(c)
    for m in range(1, inner):
        copy(stat, stat_in.at[m], sp_s.at[m], sp_r.at[m], vis=in_plane(m)).wait_recv()
    merged = combine([stat] + [stat_in.at[m] for m in range(1, inner)])
    for i in range(3):
        stat_mid[i] = merged[i]
    for step in range(1, outer):
        c = copy(stat_mid, stat_out.at[step], sz_s.at[step], sz_r.at[step], vis=on_line(step))
        c.start()
        sent.append(c)
    for step in range(1, outer):
        copy(stat_mid, stat_out.at[step], sz_s.at[step], sz_r.at[step],
             vis=on_line(step)).wait_recv()
    peak, total, weighted = combine([stat_mid] + [stat_out.at[s] for s in range(1, outer)])
    scal[0] = jnp.exp(stat[0] - peak) / total
    scal[1] = weighted / total

    def second(c, _):
        b, h = c // kv_local, lax.rem(c, kv_local)
        lanes = pl.ds(pl.multiple_of(h * HD, HD), HD)
        query = gath[0, c].reshape(rows, HD)
        grad = gath[1, c].reshape(rows, HD)
        prob = probs[c] * scal[0, pl.ds(c, 1), :]
        low = (prob * (gprobs[c] - scal[1, pl.ds(c, 1), :])).astype(jnp.bfloat16)
        dq = dot(low, k_ref[b, :, lanes], TN) * INV_ROOT
        dq_send[c] = dq.astype(jnp.bfloat16).reshape(outer, inner, GROUPS * text, HD)
        for m in range(1, inner):
            copy(dq_send.at[c, :, lax.rem(place + m, inner)], dq_plane.at[m, c],
                 rp_s.at[m, c], rp_r.at[m, c], vis=in_plane(m)).start()
        dk = dot(low, query, NN) * INV_ROOT
        dk_ref[b, :, lanes] = dk.astype(jnp.bfloat16)
        dv_ref[b, :, lanes] = dot(prob.astype(jnp.bfloat16), grad, NN).astype(jnp.bfloat16)
        return 0

    lax.fori_loop(0, chunks, second, 0)

    def arrived(c, _):
        for m in range(1, inner):
            d = copy(dq_send.at[c, :, lax.rem(place + m, inner)], dq_plane.at[m, c],
                     rp_s.at[m, c], rp_r.at[m, c], vis=in_plane(m))
            d.wait_send()
            d.wait_recv()
        return 0

    lax.fori_loop(0, chunks, arrived, 0)

    def plane_sum(owner_line):
        acc = dq_send[:, owner_line, place].astype(jnp.float32)
        for m in range(1, inner):
            acc += dq_plane[m, :, owner_line].astype(jnp.float32)
        return acc

    for step in range(1, outer):
        dq_mid[step] = plane_sum(lax.rem(line + step, outer)).astype(jnp.bfloat16)
        c = copy(dq_mid.at[step], dq_line.at[step], rz_s.at[step], rz_r.at[step], vis=on_line(step))
        c.start()
        sent.append(c)
    home = plane_sum(line)
    for step in range(1, outer):
        copy(dq_mid.at[step], dq_line.at[step], rz_s.at[step], rz_r.at[step],
             vis=on_line(step)).wait_recv()
        home += dq_line[step].astype(jnp.float32)
    for h in range(kv_local):
        for g in range(GROUPS):
            block = [home[b * kv_local + h, g * text:(g + 1) * text] for b in range(batch)]
            gath2[me, :, pl.ds((h * GROUPS + g) * HD, HD)] = jnp.concatenate(block, 0).astype(jnp.bfloat16)

    sent += gather(lambda v: gath2.at[v], hz_s, hz_r, hp_s, hp_r)

    cols = w_ref.shape[0]
    per_head = vis // heads
    product = dot(gath2[...].reshape(vis * batch * text, width), w_ref[...], NT)
    part[...] = product.reshape(heads, per_head * batch * text, cols)
    part_send[...] = product.astype(jnp.bfloat16).reshape(heads, per_head * batch * text, cols)
    for step in range(1, heads):
        c = copy(part_send.at[other_head(step)], part_in.at[step], hd_s.at[step], hd_r.at[step],
                 head=other_head(step))
        c.start()
        sent.append(c)
    mine = part[my_head]
    for step in range(1, heads):
        copy(part_send.at[other_head(step)], part_in.at[step], hd_s.at[step], hd_r.at[step],
             head=other_head(step)).wait_recv()
        mine += part_in[step].astype(jnp.float32)
    mine = mine.reshape(per_head, batch, text, cols)
    for b in range(batch):
        din_ref[b] = mine[:, b].reshape(per_head * text, cols).astype(jnp.bfloat16)
    for c in sent:
        c.wait_send()


def per_device(vis, heads, queries, keys, values, d_out, q_weight):
    batch, text, width = queries.shape
    kv_local = keys.shape[2] // HD
    chunks = batch * kv_local
    inner = math.gcd(vis, 4)
    outer = vis // inner
    block = GROUPS * text
    rows = vis * block
    tokens = keys.shape[1]
    cols = q_weight.shape[0]
    share = vis // heads * batch * text
    low, full = jnp.bfloat16, jnp.float32
    dma = pltpu.SemaphoreType.DMA
    scratch = [
        pltpu.VMEM((2, chunks, vis, block, HD), low),
        pltpu.VMEM((chunks, tokens, rows), full),
        pltpu.VMEM((chunks, tokens, rows), full),
        pltpu.VMEM((3, chunks, rows), full),
        pltpu.VMEM((inner, 3, chunks, rows), full),
        pltpu.VMEM((3, chunks, rows), full),
        pltpu.VMEM((outer, 3, chunks, rows), full),
        pltpu.VMEM((2, chunks, rows), full),
        pltpu.VMEM((chunks, outer, inner, block, HD), low),
        pltpu.VMEM((inner, chunks, outer, block, HD), low),
        pltpu.VMEM((outer, chunks, block, HD), low),
        pltpu.VMEM((outer, chunks, block, HD), low),
        pltpu.VMEM((vis, batch * text, width), low),
        pltpu.VMEM((heads, share, cols), full),
        pltpu.VMEM((heads, share, cols), low),
        pltpu.VMEM((heads, share, cols), low),
        dma((outer,)), dma((outer,)), dma((outer, inner)), dma((outer, inner)),
        dma((inner,)), dma((inner,)), dma((outer,)), dma((outer,)),
        dma((inner, chunks)), dma((inner, chunks)), dma((outer,)), dma((outer,)),
        dma((outer,)), dma((outer,)), dma((outer, inner)), dma((outer, inner)),
        dma((heads,)), dma((heads,)),
    ]
    return pl.pallas_call(
        functools.partial(kernel, outer, inner, heads),
        out_shape=(
            jax.ShapeDtypeStruct((batch, vis * text // heads, cols), low),
            jax.ShapeDtypeStruct(keys.shape, low),
            jax.ShapeDtypeStruct(values.shape, low),
        ),
        in_specs=[pl.BlockSpec(memory_space=pltpu.VMEM)] * 5,
        out_specs=(pl.BlockSpec(memory_space=pltpu.VMEM),) * 3,
        scratch_shapes=scratch,
        compiler_params=pltpu.CompilerParams(
            collective_id=0, has_side_effects=True, vmem_limit_bytes=50 * 1024 * 1024
        ),
    )(queries, d_out, keys, values, q_weight)


def solution(mesh):
    placed = (
        P(None, "vis", "head"),
        P(None, "vis", "head"),
        P(None, "vis", "head"),
        P(None, "vis", "head"),
        P("vis", "head"),
    )
    return jax.shard_map(
        functools.partial(per_device, mesh.shape["vis"], mesh.shape["head"]),
        mesh=mesh,
        in_specs=placed,
        out_specs=(P(None, "head", "vis"), P(None, "vis", "head"), P(None, "vis", "head")),
        check_vma=False,
    )
```

```python
import functools
import math

import jax
import jax.numpy as jnp
from jax import lax
from jax.experimental import pallas as pl
from jax.experimental.pallas import tpu as pltpu
from jax.sharding import PartitionSpec as P

HQ = 32
KVH = 8
HD = 128
GROUPS = HQ // KVH
INV_ROOT = HD ** (-0.5)
NT = (((1,), (1,)), ((), ()))
TN = (((0,), (0,)), ((), ()))
NN = (((1,), (0,)), ((), ()))


def dot(x, y, dims):
    return lax.dot_general(x, y, dims, preferred_element_type=jnp.float32)


def kernel(
    outer, inner, heads,
    q_hbm, g_hbm, k_hbm, v_hbm, w_hbm,
    din_ref, dk_ref, dv_ref,
    q_ref, g_ref, k_ref, v_ref, w_ref, load,
    gath, probs, gprobs, stat, stat_in, stat_mid, stat_out, scal,
    dq_send, dq_plane, dq_mid, dq_line, gath2, part, part_send, part_in,
    gz_s, gz_r, gp_s, gp_r, sp_s, sp_r, sz_s, sz_r,
    rp_s, rp_r, rz_s, rz_r, hz_s, hz_r, hp_s, hp_r, hd_s, hd_r,
):
    batch, text, width = q_ref.shape
    kv_local = width // (HD * GROUPS)
    chunks = batch * kv_local
    vis = outer * inner
    rows = vis * GROUPS * text
    me = lax.axis_index("vis")
    my_head = lax.axis_index("head")
    line, place = me // inner, lax.rem(me, inner)

    def on_line(step):
        return lax.rem(line + step + outer, outer) * inner + place

    def in_plane(step):
        return line * inner + lax.rem(place + step + inner, inner)

    def other_head(step):
        return lax.rem(my_head + step + heads, heads)

    def copy(src, dst, send, recv, **where):
        return pltpu.make_async_remote_copy(
            src_ref=src, dst_ref=dst, send_sem=send, recv_sem=recv,
            device_id=where, device_id_type=pl.DeviceIdType.MESH,
        )

    loads = [
        pltpu.make_async_copy(src, dst, load.at[i])
        for i, (src, dst) in enumerate((
            (q_hbm, q_ref), (g_hbm, g_ref), (k_hbm, k_ref), (v_hbm, v_ref), (w_hbm, w_ref)
        ))
    ]
    for d in loads:
        d.start()
    barrier = pltpu.get_barrier_semaphore()
    for step in range(1, outer):
        pl.semaphore_signal(barrier, inc=1, device_id={"vis": on_line(step)},
                            device_id_type=pl.DeviceIdType.MESH)
    for step in range(1, inner):
        pl.semaphore_signal(barrier, inc=1, device_id={"vis": in_plane(step)},
                            device_id_type=pl.DeviceIdType.MESH)
    for step in range(1, heads):
        pl.semaphore_signal(barrier, inc=1, device_id={"head": other_head(step)},
                            device_id_type=pl.DeviceIdType.MESH)
    loads[0].wait()
    loads[1].wait()
    for which, ref in ((0, q_ref), (1, g_ref)):
        for b in range(batch):
            for h in range(kv_local):
                block = [
                    ref[b, :, pl.ds((h * GROUPS + g) * HD, HD)].astype(jnp.float32)
                    for g in range(GROUPS)
                ]
                gath[which, b * kv_local + h, me] = jnp.concatenate(block, 0).astype(jnp.bfloat16)
    pl.semaphore_wait(barrier, outer + inner + heads - 3)

    def gather(slot, line_s, line_r, plane_s, plane_r):
        sent = []

        def spread(step):
            owner = on_line(-step)
            for m in range(1, inner):
                c = copy(slot(owner), slot(owner), plane_s.at[step, m], plane_r.at[step, m],
                         vis=in_plane(m))
                c.start()
                sent.append(c)

        for step in range(1, outer):
            c = copy(slot(me), slot(me), line_s.at[step], line_r.at[step], vis=on_line(step))
            c.start()
            sent.append(c)
        spread(0)
        for step in range(1, outer):
            owner = on_line(-step)
            copy(slot(owner), slot(owner), line_s.at[step], line_r.at[step],
                 vis=on_line(step)).wait_recv()
            spread(step)
        for step in range(outer):
            for m in range(1, inner):
                owner = lax.rem(line - step + outer, outer) * inner + lax.rem(place - m + inner, inner)
                copy(slot(owner), slot(owner), plane_s.at[step, m], plane_r.at[step, m],
                     vis=in_plane(m)).wait_recv()
        return sent

    sent = gather(lambda v: gath.at[:, :, v], gz_s, gz_r, gp_s, gp_r)

    loads[2].wait()
    loads[3].wait()

    def first(c, _):
        b, h = c // kv_local, lax.rem(c, kv_local)
        lanes = pl.ds(pl.multiple_of(h * HD, HD), HD)
        query = gath[0, c].reshape(rows, HD)
        grad = gath[1, c].reshape(rows, HD)
        scores = dot(k_ref[b, :, lanes], query, NT) * INV_ROOT
        peak = jnp.max(scores, axis=0, keepdims=True)
        weights = jnp.exp(scores - peak)
        grads = dot(v_ref[b, :, lanes], grad, NT)
        probs[c] = weights
        gprobs[c] = grads
        stat[0, pl.ds(c, 1), :] = peak
        stat[1, pl.ds(c, 1), :] = jnp.sum(weights, axis=0, keepdims=True)
        stat[2, pl.ds(c, 1), :] = jnp.sum(weights * grads, axis=0, keepdims=True)
        return 0

    lax.fori_loop(0, chunks, first, 0)

    def combine(parts):
        peak = functools.reduce(jnp.maximum, [p[0] for p in parts])
        scale = [jnp.exp(p[0] - peak) for p in parts]
        total = sum(p[1] * s for p, s in zip(parts, scale))
        weighted = sum(p[2] * s for p, s in zip(parts, scale))
        return peak, total, weighted

    for m in range(1, inner):
        c = copy(stat, stat_in.at[m], sp_s.at[m], sp_r.at[m], vis=in_plane(m))
        c.start()
        sent.append(c)
    for m in range(1, inner):
        copy(stat, stat_in.at[m], sp_s.at[m], sp_r.at[m], vis=in_plane(m)).wait_recv()
    merged = combine([stat] + [stat_in.at[m] for m in range(1, inner)])
    for i in range(3):
        stat_mid[i] = merged[i]
    for step in range(1, outer):
        c = copy(stat_mid, stat_out.at[step], sz_s.at[step], sz_r.at[step], vis=on_line(step))
        c.start()
        sent.append(c)
    for step in range(1, outer):
        copy(stat_mid, stat_out.at[step], sz_s.at[step], sz_r.at[step],
             vis=on_line(step)).wait_recv()
    peak, total, weighted = combine([stat_mid] + [stat_out.at[s] for s in range(1, outer)])
    scal[0] = jnp.exp(stat[0] - peak) / total
    scal[1] = weighted / total

    def second(c, _):
        b, h = c // kv_local, lax.rem(c, kv_local)
        lanes = pl.ds(pl.multiple_of(h * HD, HD), HD)
        query = gath[0, c].reshape(rows, HD)
        grad = gath[1, c].reshape(rows, HD)
        prob = probs[c] * scal[0, pl.ds(c, 1), :]
        low = (prob * (gprobs[c] - scal[1, pl.ds(c, 1), :])).astype(jnp.bfloat16)
        dq = dot(low, k_ref[b, :, lanes], TN) * INV_ROOT
        dq_send[c] = dq.astype(jnp.bfloat16).reshape(outer, inner, GROUPS * text, HD)
        for m in range(1, inner):
            copy(dq_send.at[c, :, lax.rem(place + m, inner)], dq_plane.at[m, c],
                 rp_s.at[m, c], rp_r.at[m, c], vis=in_plane(m)).start()
        dk = dot(low, query, NN) * INV_ROOT
        dk_ref[b, :, lanes] = dk.astype(jnp.bfloat16)
        dv_ref[b, :, lanes] = dot(prob.astype(jnp.bfloat16), grad, NN).astype(jnp.bfloat16)
        return 0

    lax.fori_loop(0, chunks, second, 0)

    def arrived(c, _):
        for m in range(1, inner):
            d = copy(dq_send.at[c, :, lax.rem(place + m, inner)], dq_plane.at[m, c],
                     rp_s.at[m, c], rp_r.at[m, c], vis=in_plane(m))
            d.wait_send()
            d.wait_recv()
        return 0

    lax.fori_loop(0, chunks, arrived, 0)

    def plane_sum(owner_line):
        acc = dq_send[:, owner_line, place].astype(jnp.float32)
        for m in range(1, inner):
            acc += dq_plane[m, :, owner_line].astype(jnp.float32)
        return acc

    for step in range(1, outer):
        dq_mid[step] = plane_sum(lax.rem(line + step, outer)).astype(jnp.bfloat16)
        c = copy(dq_mid.at[step], dq_line.at[step], rz_s.at[step], rz_r.at[step], vis=on_line(step))
        c.start()
        sent.append(c)
    home = plane_sum(line)
    for step in range(1, outer):
        copy(dq_mid.at[step], dq_line.at[step], rz_s.at[step], rz_r.at[step],
             vis=on_line(step)).wait_recv()
        home += dq_line[step].astype(jnp.float32)
    for h in range(kv_local):
        for g in range(GROUPS):
            block = [home[b * kv_local + h, g * text:(g + 1) * text] for b in range(batch)]
            gath2[me, :, pl.ds((h * GROUPS + g) * HD, HD)] = jnp.concatenate(block, 0).astype(jnp.bfloat16)

    sent += gather(lambda v: gath2.at[v], hz_s, hz_r, hp_s, hp_r)

    loads[4].wait()
    cols = w_ref.shape[0]
    per_head = vis // heads
    product = dot(gath2[...].reshape(vis * batch * text, width), w_ref[...], NT)
    part[...] = product.reshape(heads, per_head * batch * text, cols)
    part_send[...] = product.astype(jnp.bfloat16).reshape(heads, per_head * batch * text, cols)
    for step in range(1, heads):
        c = copy(part_send.at[other_head(step)], part_in.at[step], hd_s.at[step], hd_r.at[step],
                 head=other_head(step))
        c.start()
        sent.append(c)
    mine = part[my_head]
    for step in range(1, heads):
        copy(part_send.at[other_head(step)], part_in.at[step], hd_s.at[step], hd_r.at[step],
             head=other_head(step)).wait_recv()
        mine += part_in[step].astype(jnp.float32)
    mine = mine.reshape(per_head, batch, text, cols)
    for b in range(batch):
        din_ref[b] = mine[:, b].reshape(per_head * text, cols).astype(jnp.bfloat16)
    for c in sent:
        c.wait_send()


def per_device(vis, heads, queries, keys, values, d_out, q_weight):
    batch, text, width = queries.shape
    kv_local = keys.shape[2] // HD
    chunks = batch * kv_local
    inner = math.gcd(vis, 4)
    outer = vis // inner
    block = GROUPS * text
    rows = vis * block
    tokens = keys.shape[1]
    cols = q_weight.shape[0]
    share = vis // heads * batch * text
    low, full = jnp.bfloat16, jnp.float32
    dma = pltpu.SemaphoreType.DMA
    scratch = [
        pltpu.VMEM(queries.shape, low),
        pltpu.VMEM(d_out.shape, low),
        pltpu.VMEM(keys.shape, low),
        pltpu.VMEM(values.shape, low),
        pltpu.VMEM(q_weight.shape, low),
        dma((5,)),
        pltpu.VMEM((2, chunks, vis, block, HD), low),
        pltpu.VMEM((chunks, tokens, rows), full),
        pltpu.VMEM((chunks, tokens, rows), full),
        pltpu.VMEM((3, chunks, rows), full),
        pltpu.VMEM((inner, 3, chunks, rows), full),
        pltpu.VMEM((3, chunks, rows), full),
        pltpu.VMEM((outer, 3, chunks, rows), full),
        pltpu.VMEM((2, chunks, rows), full),
        pltpu.VMEM((chunks, outer, inner, block, HD), low),
        pltpu.VMEM((inner, chunks, outer, block, HD), low),
        pltpu.VMEM((outer, chunks, block, HD), low),
        pltpu.VMEM((outer, chunks, block, HD), low),
        pltpu.VMEM((vis, batch * text, width), low),
        pltpu.VMEM((heads, share, cols), full),
        pltpu.VMEM((heads, share, cols), low),
        pltpu.VMEM((heads, share, cols), low),
        dma((outer,)), dma((outer,)), dma((outer, inner)), dma((outer, inner)),
        dma((inner,)), dma((inner,)), dma((outer,)), dma((outer,)),
        dma((inner, chunks)), dma((inner, chunks)), dma((outer,)), dma((outer,)),
        dma((outer,)), dma((outer,)), dma((outer, inner)), dma((outer, inner)),
        dma((heads,)), dma((heads,)),
    ]
    return pl.pallas_call(
        functools.partial(kernel, outer, inner, heads),
        out_shape=(
            jax.ShapeDtypeStruct((batch, vis * text // heads, cols), low),
            jax.ShapeDtypeStruct(keys.shape, low),
            jax.ShapeDtypeStruct(values.shape, low),
        ),
        in_specs=[pl.BlockSpec(memory_space=pltpu.HBM)] * 5,
        out_specs=(pl.BlockSpec(memory_space=pltpu.VMEM),) * 3,
        scratch_shapes=scratch,
        compiler_params=pltpu.CompilerParams(
            collective_id=0, has_side_effects=True, vmem_limit_bytes=50 * 1024 * 1024
        ),
    )(queries, d_out, keys, values, q_weight)


def solution(mesh):
    placed = (
        P(None, "vis", "head"),
        P(None, "vis", "head"),
        P(None, "vis", "head"),
        P(None, "vis", "head"),
        P("vis", "head"),
    )
    return jax.shard_map(
        functools.partial(per_device, mesh.shape["vis"], mesh.shape["head"]),
        mesh=mesh,
        in_specs=placed,
        out_specs=(P(None, "head", "vis"), P(None, "vis", "head"), P(None, "vis", "head")),
        check_vma=False,
    )
```

```python
import functools
import math

import jax
import jax.numpy as jnp
from jax import lax
from jax.experimental import pallas as pl
from jax.experimental.pallas import tpu as pltpu
from jax.sharding import PartitionSpec as P

HQ = 32
KVH = 8
HD = 128
GROUPS = HQ // KVH
INV_ROOT = HD ** (-0.5)
NT = (((1,), (1,)), ((), ()))
TN = (((0,), (0,)), ((), ()))
NN = (((1,), (0,)), ((), ()))


def dot(x, y, dims):
    return lax.dot_general(x, y, dims, preferred_element_type=jnp.float32)


def kernel(
    outer, inner, heads,
    q_hbm, g_hbm, k_hbm, v_hbm, w_hbm,
    din_ref, dk_hbm, dv_hbm,
    dk_ref, dv_ref, store,
    q_ref, g_ref, k_ref, v_ref, w_ref, load,
    gath, probs, gprobs, stat, stat_in, stat_mid, stat_out, final, scal,
    dq_send, dq_plane, dq_mid, dq_line, gath2, part, part_send, part_in,
    gz_s, gz_r, gp_s, gp_r, sp_s, sp_r, sz_s, sz_r, sf_s, sf_r,
    rp_s, rp_r, rz_s, rz_r, hz_s, hz_r, hp_s, hp_r, hd_s, hd_r,
):
    batch, text, width = q_ref.shape
    kv_local = width // (HD * GROUPS)
    chunks = batch * kv_local
    vis = outer * inner
    rows = vis * GROUPS * text
    me = lax.axis_index("vis")
    my_head = lax.axis_index("head")
    line, place = me // inner, lax.rem(me, inner)

    def on_line(step):
        return lax.rem(line + step + outer, outer) * inner + place

    def in_plane(step):
        return line * inner + lax.rem(place + step + inner, inner)

    def other_head(step):
        return lax.rem(my_head + step + heads, heads)

    def copy(src, dst, send, recv, **where):
        return pltpu.make_async_remote_copy(
            src_ref=src, dst_ref=dst, send_sem=send, recv_sem=recv,
            device_id=where, device_id_type=pl.DeviceIdType.MESH,
        )

    loads = [
        pltpu.make_async_copy(src, dst, load.at[i])
        for i, (src, dst) in enumerate((
            (q_hbm, q_ref), (g_hbm, g_ref), (k_hbm, k_ref), (v_hbm, v_ref), (w_hbm, w_ref)
        ))
    ]
    for d in loads:
        d.start()
    barrier = pltpu.get_barrier_semaphore()
    for step in range(1, outer):
        pl.semaphore_signal(barrier, inc=1, device_id={"vis": on_line(step)},
                            device_id_type=pl.DeviceIdType.MESH)
    for step in range(1, inner):
        pl.semaphore_signal(barrier, inc=1, device_id={"vis": in_plane(step)},
                            device_id_type=pl.DeviceIdType.MESH)
    for step in range(1, heads):
        pl.semaphore_signal(barrier, inc=1, device_id={"head": other_head(step)},
                            device_id_type=pl.DeviceIdType.MESH)
    loads[0].wait()
    loads[1].wait()
    for which, ref in ((0, q_ref), (1, g_ref)):
        for b in range(batch):
            for h in range(kv_local):
                block = [
                    ref[b, :, pl.ds((h * GROUPS + g) * HD, HD)].astype(jnp.float32)
                    for g in range(GROUPS)
                ]
                gath[which, b * kv_local + h, me] = jnp.concatenate(block, 0).astype(jnp.bfloat16)
    pl.semaphore_wait(barrier, outer + inner + heads - 3)

    def flip(bit):
        return line * inner + place + bit * (1 - 2 * lax.rem(place // bit, 2))

    def gather(slot, line_s, line_r, plane_s, plane_r):
        sent = []

        def owner_of(step, bits):
            column = place
            for bit in bits:
                column = column + bit * (1 - 2 * lax.rem(place // bit, 2))
            return lax.rem(line - step + outer, outer) * inner + column

        def plane_copy(step, i, owner, half, bit):
            return copy(slot(owner, half), slot(owner, half), plane_s.at[step, i],
                        plane_r.at[step, i], vis=flip(bit))

        def begin(c):
            c.start()
            sent.append(c)

        def line_copy(step, owner, half):
            return copy(slot(owner, half), slot(owner, half), line_s.at[step, half],
                        line_r.at[step, half], vis=on_line(step))

        def spread(step):
            owner = owner_of(step, ())
            for half, bit in ((0, 1), (1, 2), (1, 1), (0, 2)):
                begin(plane_copy(step, half + 2 * (bit - 1), owner, half, bit))

        def relay(step):
            plane_copy(step, 0, owner_of(step, (1,)), 0, 1).wait_recv()
            begin(plane_copy(step, 4, owner_of(step, (1,)), 0, 2))
            plane_copy(step, 3, owner_of(step, (2,)), 1, 2).wait_recv()
            begin(plane_copy(step, 5, owner_of(step, (2,)), 1, 1))

        for step in range(1, outer):
            for half in range(2):
                begin(line_copy(step, me, half))
        spread(0)
        for step in range(1, outer):
            for half in range(2):
                line_copy(step, owner_of(step, ()), half).wait_recv()
            spread(step)
            relay(step - 1)
        relay(outer - 1)
        for step in range(outer):
            plane_copy(step, 1, owner_of(step, (1,)), 1, 1).wait_recv()
            plane_copy(step, 2, owner_of(step, (2,)), 0, 2).wait_recv()
            plane_copy(step, 4, owner_of(step, (1, 2)), 0, 2).wait_recv()
            plane_copy(step, 5, owner_of(step, (1, 2)), 1, 1).wait_recv()
        return sent

    sent = gather(lambda v, half: gath.at[half, :, v], gz_s, gz_r, gp_s, gp_r)

    loads[2].wait()
    loads[3].wait()

    def first(c, _):
        b, h = c // kv_local, lax.rem(c, kv_local)
        lanes = pl.ds(pl.multiple_of(h * HD, HD), HD)
        query = gath[0, c].reshape(rows, HD)
        grad = gath[1, c].reshape(rows, HD)
        scores = dot(k_ref[b, :, lanes], query, NT) * INV_ROOT
        peak = jnp.max(scores, axis=0, keepdims=True)
        weights = jnp.exp(scores - peak)
        grads = dot(v_ref[b, :, lanes], grad, NT)
        probs[c] = weights
        gprobs[c] = grads
        stat[0, pl.ds(c, 1), :] = peak
        stat[1, pl.ds(c, 1), :] = jnp.sum(weights, axis=0, keepdims=True)
        stat[2, pl.ds(c, 1), :] = jnp.sum(weights * grads, axis=0, keepdims=True)
        return 0

    lax.fori_loop(0, chunks, first, 0)

    def combine(parts):
        peak = functools.reduce(jnp.maximum, [p[0] for p in parts])
        scale = [jnp.exp(p[0] - peak) for p in parts]
        total = sum(p[1] * s for p, s in zip(parts, scale))
        weighted = sum(p[2] * s for p, s in zip(parts, scale))
        return peak, total, weighted

    span = rows // inner

    def lanes_of(step):
        return pl.ds(pl.multiple_of(lax.rem(place + step + inner, inner) * span, span), span)

    def plane_stat(m):
        return copy(stat.at[:, :, lanes_of(m)], stat_in.at[m], sp_s.at[m], sp_r.at[m], vis=in_plane(m))

    def line_stat(step):
        return copy(stat_mid, stat_out.at[step], sz_s.at[step], sz_r.at[step], vis=on_line(step))

    def final_stat(m, lanes):
        return copy(final.at[:, :, lanes], final.at[:, :, lanes], sf_s.at[m], sf_r.at[m], vis=in_plane(m))

    for m in range(1, inner):
        c = plane_stat(m)
        c.start()
        sent.append(c)
    stat_in[0] = stat[:, :, lanes_of(0)]
    for m in range(1, inner):
        plane_stat(m).wait_recv()
    merged = combine([stat_in.at[m] for m in range(inner)])
    for i in range(3):
        stat_mid[i] = merged[i]
    for step in range(1, outer):
        c = line_stat(step)
        c.start()
        sent.append(c)
    for step in range(1, outer):
        line_stat(step).wait_recv()
    peak, total, weighted = combine([stat_mid] + [stat_out.at[s] for s in range(1, outer)])
    final[0, :, lanes_of(0)] = peak + jnp.log(total)
    final[1, :, lanes_of(0)] = weighted / total
    for m in range(1, inner):
        c = final_stat(m, lanes_of(0))
        c.start()
        sent.append(c)
    for m in range(1, inner):
        final_stat(m, lanes_of(-m)).wait_recv()
    scal[0] = jnp.exp(stat[0] - final[0])
    scal[1] = final[1]

    def second(c, _):
        b, h = c // kv_local, lax.rem(c, kv_local)
        lanes = pl.ds(pl.multiple_of(h * HD, HD), HD)
        query = gath[0, c].reshape(rows, HD)
        grad = gath[1, c].reshape(rows, HD)
        prob = probs[c] * scal[0, pl.ds(c, 1), :]
        low = (prob * (gprobs[c] - scal[1, pl.ds(c, 1), :])).astype(jnp.bfloat16)
        dq = dot(low, k_ref[b, :, lanes], TN) * INV_ROOT
        dq_send[c] = dq.astype(jnp.bfloat16).reshape(outer, inner, GROUPS * text, HD)
        for m in range(1, inner):
            copy(dq_send.at[c, :, lax.rem(place + m, inner)], dq_plane.at[m, c],
                 rp_s.at[m, c], rp_r.at[m, c], vis=in_plane(m)).start()
        dk = dot(low, query, NN) * INV_ROOT
        dk_ref[b, :, lanes] = dk.astype(jnp.bfloat16)
        dv_ref[b, :, lanes] = dot(prob.astype(jnp.bfloat16), grad, NN).astype(jnp.bfloat16)
        return 0

    lax.fori_loop(0, chunks, second, 0)

    saves = [
        pltpu.make_async_copy(dk_ref, dk_hbm, store.at[0]),
        pltpu.make_async_copy(dv_ref, dv_hbm, store.at[1]),
    ]
    for d in saves:
        d.start()

    def arrived(c, _):
        for m in range(1, inner):
            d = copy(dq_send.at[c, :, lax.rem(place + m, inner)], dq_plane.at[m, c],
                     rp_s.at[m, c], rp_r.at[m, c], vis=in_plane(m))
            d.wait_send()
            d.wait_recv()
        return 0

    lax.fori_loop(0, chunks, arrived, 0)

    def plane_sum(owner_line):
        acc = dq_send[:, owner_line, place].astype(jnp.float32)
        for m in range(1, inner):
            acc += dq_plane[m, :, owner_line].astype(jnp.float32)
        return acc

    for step in range(1, outer):
        dq_mid[step] = plane_sum(lax.rem(line + step, outer)).astype(jnp.bfloat16)
        c = copy(dq_mid.at[step], dq_line.at[step], rz_s.at[step], rz_r.at[step], vis=on_line(step))
        c.start()
        sent.append(c)
    home = plane_sum(line)
    for step in range(1, outer):
        copy(dq_mid.at[step], dq_line.at[step], rz_s.at[step], rz_r.at[step],
             vis=on_line(step)).wait_recv()
        home += dq_line[step].astype(jnp.float32)
    for h in range(kv_local):
        for g in range(GROUPS):
            block = [home[b * kv_local + h, g * text:(g + 1) * text] for b in range(batch)]
            gath2[me, :, pl.ds((h * GROUPS + g) * HD, HD)] = jnp.concatenate(block, 0).astype(jnp.bfloat16)

    sent += gather(lambda v, half: gath2.at[v, :, pl.ds(half * (width // 2), width // 2)], hz_s, hz_r, hp_s, hp_r)

    loads[4].wait()
    cols = w_ref.shape[0]
    per_head = vis // heads
    product = dot(gath2[...].reshape(vis * batch * text, width), w_ref[...], NT)
    part[...] = product.reshape(heads, per_head * batch * text, cols)
    part_send[...] = product.astype(jnp.bfloat16).reshape(heads, per_head * batch * text, cols)
    for step in range(1, heads):
        c = copy(part_send.at[other_head(step)], part_in.at[step], hd_s.at[step], hd_r.at[step],
                 head=other_head(step))
        c.start()
        sent.append(c)
    mine = part[my_head]
    for step in range(1, heads):
        copy(part_send.at[other_head(step)], part_in.at[step], hd_s.at[step], hd_r.at[step],
             head=other_head(step)).wait_recv()
        mine += part_in[step].astype(jnp.float32)
    mine = mine.reshape(per_head, batch, text, cols)
    for b in range(batch):
        din_ref[b] = mine[:, b].reshape(per_head * text, cols).astype(jnp.bfloat16)
    for c in sent:
        c.wait_send()
    for d in saves:
        d.wait()


def leave(*refs):
    count = len(refs) // 2
    moves = [pltpu.make_async_copy(refs[i], refs[count + i], refs[-1].at[i]) for i in range(count)]
    for d in moves:
        d.start()
    for d in moves:
        d.wait()


def per_device(vis, heads, queries, keys, values, d_out, q_weight):
    batch, text, width = queries.shape
    kv_local = keys.shape[2] // HD
    chunks = batch * kv_local
    inner = math.gcd(vis, 4)
    outer = vis // inner
    block = GROUPS * text
    rows = vis * block
    tokens = keys.shape[1]
    cols = q_weight.shape[0]
    share = vis // heads * batch * text
    low, full = jnp.bfloat16, jnp.float32
    dma = pltpu.SemaphoreType.DMA
    scratch = [
        pltpu.VMEM(keys.shape, low),
        pltpu.VMEM(values.shape, low),
        dma((2,)),
        pltpu.VMEM(queries.shape, low),
        pltpu.VMEM(d_out.shape, low),
        pltpu.VMEM(keys.shape, low),
        pltpu.VMEM(values.shape, low),
        pltpu.VMEM(q_weight.shape, low),
        dma((5,)),
        pltpu.VMEM((2, chunks, vis, block, HD), low),
        pltpu.VMEM((chunks, tokens, rows), full),
        pltpu.VMEM((chunks, tokens, rows), full),
        pltpu.VMEM((3, chunks, rows), full),
        pltpu.VMEM((inner, 3, chunks, rows // inner), full),
        pltpu.VMEM((3, chunks, rows // inner), full),
        pltpu.VMEM((outer, 3, chunks, rows // inner), full),
        pltpu.VMEM((2, chunks, rows), full),
        pltpu.VMEM((2, chunks, rows), full),
        pltpu.VMEM((chunks, outer, inner, block, HD), low),
        pltpu.VMEM((inner, chunks, outer, block, HD), low),
        pltpu.VMEM((outer, chunks, block, HD), low),
        pltpu.VMEM((outer, chunks, block, HD), low),
        pltpu.VMEM((vis, batch * text, width), low),
        pltpu.VMEM((heads, share, cols), full),
        pltpu.VMEM((heads, share, cols), low),
        pltpu.VMEM((heads, share, cols), low),
        dma((outer, 2)), dma((outer, 2)), dma((outer, 6)), dma((outer, 6)),
        dma((inner,)), dma((inner,)), dma((outer,)), dma((outer,)), dma((inner,)), dma((inner,)),
        dma((inner, chunks)), dma((inner, chunks)), dma((outer,)), dma((outer,)),
        dma((outer, 2)), dma((outer, 2)), dma((outer, 6)), dma((outer, 6)),
        dma((heads,)), dma((heads,)),
    ]
    results = pl.pallas_call(
        functools.partial(kernel, outer, inner, heads),
        out_shape=(
            jax.ShapeDtypeStruct((batch, vis * text // heads, cols), low),
            jax.ShapeDtypeStruct(keys.shape, low),
            jax.ShapeDtypeStruct(values.shape, low),
        ),
        in_specs=[pl.BlockSpec(memory_space=pltpu.HBM)] * 5,
        out_specs=(pl.BlockSpec(memory_space=pltpu.VMEM),) + (pl.BlockSpec(memory_space=pltpu.HBM),) * 2,
        scratch_shapes=scratch,
        compiler_params=pltpu.CompilerParams(
            collective_id=0, has_side_effects=True, vmem_limit_bytes=60 * 1024 * 1024
        ),
    )(queries, d_out, keys, values, q_weight)
    return pl.pallas_call(
        leave,
        out_shape=tuple(jax.ShapeDtypeStruct(x.shape, x.dtype) for x in results),
        in_specs=[pl.BlockSpec(memory_space=pltpu.VMEM)] * len(results),
        out_specs=(pl.BlockSpec(memory_space=pltpu.HBM),) * len(results),
        scratch_shapes=[dma((len(results),))],
    )(*results)


def solution(mesh):
    placed = (
        P(None, "vis", "head"),
        P(None, "vis", "head"),
        P(None, "vis", "head"),
        P(None, "vis", "head"),
        P("vis", "head"),
    )
    return jax.shard_map(
        functools.partial(per_device, mesh.shape["vis"], mesh.shape["head"]),
        mesh=mesh,
        in_specs=placed,
        out_specs=(P(None, "head", "vis"), P(None, "vis", "head"), P(None, "vis", "head")),
        check_vma=False,
    )
```

```python
import functools
import math

import jax
import jax.numpy as jnp
from jax import lax
from jax.experimental import pallas as pl
from jax.experimental.pallas import tpu as pltpu
from jax.sharding import PartitionSpec as P

HQ = 32
KVH = 8
HD = 128
GROUPS = HQ // KVH
INV_ROOT = HD ** (-0.5)
NT = (((1,), (1,)), ((), ()))
TN = (((0,), (0,)), ((), ()))
NN = (((1,), (0,)), ((), ()))


def dot(x, y, dims):
    return lax.dot_general(x, y, dims, preferred_element_type=jnp.float32)


def kernel(
    outer, inner, heads,
    q_hbm, g_hbm, k_hbm, v_hbm, w_hbm,
    din_ref, dk_hbm, dv_hbm,
    dk_ref, dv_ref, store,
    q_ref, g_ref, k_ref, v_ref, w_ref, load,
    gath, probs, gprobs, stat, stat_in, stat_mid, stat_out, final, scal,
    dq_send, dq_plane, dq_mid, dq_line, gath2, part, part_send, part_in,
    gz_s, gz_r, gp_s, gp_r, sp_s, sp_r, sz_s, sz_r, sf_s, sf_r,
    rp_s, rp_r, rz_s, rz_r, hz_s, hz_r, hp_s, hp_r, hd_s, hd_r,
):
    batch, text, width = q_ref.shape
    kv_local = width // (HD * GROUPS)
    chunks = batch * kv_local
    vis = outer * inner
    rows = vis * GROUPS * text
    me = lax.axis_index("vis")
    my_head = lax.axis_index("head")
    line, place = me // inner, lax.rem(me, inner)

    def on_line(step):
        return lax.rem(line + step + outer, outer) * inner + place

    def in_plane(step):
        return line * inner + lax.rem(place + step + inner, inner)

    def other_head(step):
        return lax.rem(my_head + step + heads, heads)

    def copy(src, dst, send, recv, **where):
        return pltpu.make_async_remote_copy(
            src_ref=src, dst_ref=dst, send_sem=send, recv_sem=recv,
            device_id=where, device_id_type=pl.DeviceIdType.MESH,
        )

    loads = [
        pltpu.make_async_copy(src, dst, load.at[i])
        for i, (src, dst) in enumerate((
            (q_hbm, q_ref), (g_hbm, g_ref), (k_hbm, k_ref), (v_hbm, v_ref), (w_hbm, w_ref)
        ))
    ]
    for d in loads:
        d.start()
    barrier = pltpu.get_barrier_semaphore()
    for step in range(1, outer):
        pl.semaphore_signal(barrier, inc=1, device_id={"vis": on_line(step)},
                            device_id_type=pl.DeviceIdType.MESH)
    for step in range(1, inner):
        pl.semaphore_signal(barrier, inc=1, device_id={"vis": in_plane(step)},
                            device_id_type=pl.DeviceIdType.MESH)
    for step in range(1, heads):
        pl.semaphore_signal(barrier, inc=1, device_id={"head": other_head(step)},
                            device_id_type=pl.DeviceIdType.MESH)
    loads[0].wait()
    loads[1].wait()
    for which, ref in ((0, q_ref), (1, g_ref)):
        for b in range(batch):
            for h in range(kv_local):
                block = [
                    ref[b, :, pl.ds((h * GROUPS + g) * HD, HD)].astype(jnp.float32)
                    for g in range(GROUPS)
                ]
                gath[which, b * kv_local + h, me] = jnp.concatenate(block, 0).astype(jnp.bfloat16)
    pl.semaphore_wait(barrier, outer + inner + heads - 3)

    def flip(bit):
        return line * inner + place + bit * (1 - 2 * lax.rem(place // bit, 2))

    def gather(slot, line_s, line_r, plane_s, plane_r):
        sent = []

        def owner_of(step, bits):
            column = place
            for bit in bits:
                column = column + bit * (1 - 2 * lax.rem(place // bit, 2))
            return lax.rem(line - step + outer, outer) * inner + column

        def plane_copy(step, i, owner, half, bit):
            return copy(slot(owner, half), slot(owner, half), plane_s.at[step, i],
                        plane_r.at[step, i], vis=flip(bit))

        def begin(c):
            c.start()
            sent.append(c)

        def line_copy(step, owner, half):
            return copy(slot(owner, half), slot(owner, half), line_s.at[step, half],
                        line_r.at[step, half], vis=on_line(step))

        def spread(step):
            owner = owner_of(step, ())
            for half, bit in ((0, 1), (1, 2), (1, 1), (0, 2)):
                begin(plane_copy(step, half + 2 * (bit - 1), owner, half, bit))

        def relay(step):
            plane_copy(step, 0, owner_of(step, (1,)), 0, 1).wait_recv()
            begin(plane_copy(step, 4, owner_of(step, (1,)), 0, 2))
            plane_copy(step, 3, owner_of(step, (2,)), 1, 2).wait_recv()
            begin(plane_copy(step, 5, owner_of(step, (2,)), 1, 1))

        for step in range(1, outer):
            for half in range(2):
                begin(line_copy(step, me, half))
        spread(0)

        def forward():
            for step in range(1, outer):
                for half in range(2):
                    line_copy(step, owner_of(step, ()), half).wait_recv()
                spread(step)
                relay(step - 1)
            relay(outer - 1)

        def finish():
            for step in range(outer):
                finish_step(step)

        def finish_step(step):
            plane_copy(step, 1, owner_of(step, (1,)), 1, 1).wait_recv()
            plane_copy(step, 2, owner_of(step, (2,)), 0, 2).wait_recv()
            plane_copy(step, 4, owner_of(step, (1, 2)), 0, 2).wait_recv()
            plane_copy(step, 5, owner_of(step, (1, 2)), 1, 1).wait_recv()
        return sent, forward, finish

    sent = []
    gathers = []
    for b in range(batch):
        mine = pl.ds(b * kv_local, kv_local)
        gathers.append(gather(
            lambda v, half, mine=mine: gath.at[half, mine, v],
            gz_s.at[b], gz_r.at[b], gp_s.at[b], gp_r.at[b],
        ))
    for more, forward, finish in gathers:
        forward()
        sent += more

    loads[2].wait()
    loads[3].wait()

    def first(c, _):
        b, h = c // kv_local, lax.rem(c, kv_local)
        lanes = pl.ds(pl.multiple_of(h * HD, HD), HD)
        query = gath[0, c].reshape(rows, HD)
        grad = gath[1, c].reshape(rows, HD)
        scores = dot(k_ref[b, :, lanes], query, NT) * INV_ROOT
        peak = jnp.max(scores, axis=0, keepdims=True)
        weights = jnp.exp(scores - peak)
        grads = dot(v_ref[b, :, lanes], grad, NT)
        probs[c] = weights
        gprobs[c] = grads
        stat[0, pl.ds(c, 1), :] = peak
        stat[1, pl.ds(c, 1), :] = jnp.sum(weights, axis=0, keepdims=True)
        stat[2, pl.ds(c, 1), :] = jnp.sum(weights * grads, axis=0, keepdims=True)
        return 0

    for b in range(batch):
        gathers[b][2]()
        lax.fori_loop(b * kv_local, (b + 1) * kv_local, first, 0)

    def combine(parts):
        peak = functools.reduce(jnp.maximum, [p[0] for p in parts])
        scale = [jnp.exp(p[0] - peak) for p in parts]
        total = sum(p[1] * s for p, s in zip(parts, scale))
        weighted = sum(p[2] * s for p, s in zip(parts, scale))
        return peak, total, weighted

    span = rows // inner

    def lanes_of(step):
        return pl.ds(pl.multiple_of(lax.rem(place + step + inner, inner) * span, span), span)

    def plane_stat(m):
        return copy(stat.at[:, :, lanes_of(m)], stat_in.at[m], sp_s.at[m], sp_r.at[m], vis=in_plane(m))

    def line_stat(step):
        return copy(stat_mid, stat_out.at[step], sz_s.at[step], sz_r.at[step], vis=on_line(step))

    def final_stat(m, lanes):
        return copy(final.at[:, :, lanes], final.at[:, :, lanes], sf_s.at[m], sf_r.at[m], vis=in_plane(m))

    for m in range(1, inner):
        c = plane_stat(m)
        c.start()
        sent.append(c)
    stat_in[0] = stat[:, :, lanes_of(0)]
    for m in range(1, inner):
        plane_stat(m).wait_recv()
    merged = combine([stat_in.at[m] for m in range(inner)])
    for i in range(3):
        stat_mid[i] = merged[i]
    for step in range(1, outer):
        c = line_stat(step)
        c.start()
        sent.append(c)
    for step in range(1, outer):
        line_stat(step).wait_recv()
    peak, total, weighted = combine([stat_mid] + [stat_out.at[s] for s in range(1, outer)])
    final[0, :, lanes_of(0)] = peak + jnp.log(total)
    final[1, :, lanes_of(0)] = weighted / total
    for m in range(1, inner):
        c = final_stat(m, lanes_of(0))
        c.start()
        sent.append(c)
    for m in range(1, inner):
        final_stat(m, lanes_of(-m)).wait_recv()
    scal[0] = jnp.exp(stat[0] - final[0])
    scal[1] = final[1]

    def second(c, _):
        b, h = c // kv_local, lax.rem(c, kv_local)
        lanes = pl.ds(pl.multiple_of(h * HD, HD), HD)
        query = gath[0, c].reshape(rows, HD)
        grad = gath[1, c].reshape(rows, HD)
        prob = probs[c] * scal[0, pl.ds(c, 1), :]
        low = (prob * (gprobs[c] - scal[1, pl.ds(c, 1), :])).astype(jnp.bfloat16)
        dq = dot(low, k_ref[b, :, lanes], TN) * INV_ROOT
        dq_send[c] = dq.astype(jnp.bfloat16).reshape(outer, inner, GROUPS * text, HD)
        for m in range(1, inner):
            copy(dq_send.at[c, :, lax.rem(place + m, inner)], dq_plane.at[m, c],
                 rp_s.at[m, c], rp_r.at[m, c], vis=in_plane(m)).start()
        dk = dot(low, query, NN) * INV_ROOT
        dk_ref[b, :, lanes] = dk.astype(jnp.bfloat16)
        dv_ref[b, :, lanes] = dot(prob.astype(jnp.bfloat16), grad, NN).astype(jnp.bfloat16)
        return 0

    lax.fori_loop(0, chunks, second, 0)

    saves = [
        pltpu.make_async_copy(dk_ref, dk_hbm, store.at[0]),
        pltpu.make_async_copy(dv_ref, dv_hbm, store.at[1]),
    ]
    for d in saves:
        d.start()

    def arrived(c, _):
        for m in range(1, inner):
            d = copy(dq_send.at[c, :, lax.rem(place + m, inner)], dq_plane.at[m, c],
                     rp_s.at[m, c], rp_r.at[m, c], vis=in_plane(m))
            d.wait_send()
            d.wait_recv()
        return 0

    lax.fori_loop(0, chunks, arrived, 0)

    def plane_sum(owner_line):
        acc = dq_send[:, owner_line, place].astype(jnp.float32)
        for m in range(1, inner):
            acc += dq_plane[m, :, owner_line].astype(jnp.float32)
        return acc

    for step in range(1, outer):
        dq_mid[step] = plane_sum(lax.rem(line + step, outer)).astype(jnp.bfloat16)
        c = copy(dq_mid.at[step], dq_line.at[step], rz_s.at[step], rz_r.at[step], vis=on_line(step))
        c.start()
        sent.append(c)
    home = plane_sum(line)
    for step in range(1, outer):
        copy(dq_mid.at[step], dq_line.at[step], rz_s.at[step], rz_r.at[step],
             vis=on_line(step)).wait_recv()
        home += dq_line[step].astype(jnp.float32)
    for h in range(kv_local):
        for g in range(GROUPS):
            block = [home[b * kv_local + h, g * text:(g + 1) * text] for b in range(batch)]
            gath2[me, :, pl.ds((h * GROUPS + g) * HD, HD)] = jnp.concatenate(block, 0).astype(jnp.bfloat16)

    more, forward, finish = gather(lambda v, half: gath2.at[v, :, pl.ds(half * (width // 2), width // 2)], hz_s, hz_r, hp_s, hp_r)
    forward()
    sent += more
    finish()

    loads[4].wait()
    cols = w_ref.shape[0]
    per_head = vis // heads
    product = dot(gath2[...].reshape(vis * batch * text, width), w_ref[...], NT)
    part[...] = product.reshape(heads, per_head * batch * text, cols)
    part_send[...] = product.astype(jnp.bfloat16).reshape(heads, per_head * batch * text, cols)
    for step in range(1, heads):
        c = copy(part_send.at[other_head(step)], part_in.at[step], hd_s.at[step], hd_r.at[step],
                 head=other_head(step))
        c.start()
        sent.append(c)
    mine = part[my_head]
    for step in range(1, heads):
        copy(part_send.at[other_head(step)], part_in.at[step], hd_s.at[step], hd_r.at[step],
             head=other_head(step)).wait_recv()
        mine += part_in[step].astype(jnp.float32)
    mine = mine.reshape(per_head, batch, text, cols)
    for b in range(batch):
        din_ref[b] = mine[:, b].reshape(per_head * text, cols).astype(jnp.bfloat16)
    for c in sent:
        c.wait_send()
    for d in saves:
        d.wait()


def leave(*refs):
    count = len(refs) // 2
    moves = [pltpu.make_async_copy(refs[i], refs[count + i], refs[-1].at[i]) for i in range(count)]
    for d in moves:
        d.start()
    for d in moves:
        d.wait()


def per_device(vis, heads, queries, keys, values, d_out, q_weight):
    batch, text, width = queries.shape
    kv_local = keys.shape[2] // HD
    chunks = batch * kv_local
    inner = math.gcd(vis, 4)
    outer = vis // inner
    block = GROUPS * text
    rows = vis * block
    tokens = keys.shape[1]
    cols = q_weight.shape[0]
    share = vis // heads * batch * text
    low, full = jnp.bfloat16, jnp.float32
    dma = pltpu.SemaphoreType.DMA
    scratch = [
        pltpu.VMEM(keys.shape, low),
        pltpu.VMEM(values.shape, low),
        dma((2,)),
        pltpu.VMEM(queries.shape, low),
        pltpu.VMEM(d_out.shape, low),
        pltpu.VMEM(keys.shape, low),
        pltpu.VMEM(values.shape, low),
        pltpu.VMEM(q_weight.shape, low),
        dma((5,)),
        pltpu.VMEM((2, chunks, vis, block, HD), low),
        pltpu.VMEM((chunks, tokens, rows), full),
        pltpu.VMEM((chunks, tokens, rows), full),
        pltpu.VMEM((3, chunks, rows), full),
        pltpu.VMEM((inner, 3, chunks, rows // inner), full),
        pltpu.VMEM((3, chunks, rows // inner), full),
        pltpu.VMEM((outer, 3, chunks, rows // inner), full),
        pltpu.VMEM((2, chunks, rows), full),
        pltpu.VMEM((2, chunks, rows), full),
        pltpu.VMEM((chunks, outer, inner, block, HD), low),
        pltpu.VMEM((inner, chunks, outer, block, HD), low),
        pltpu.VMEM((outer, chunks, block, HD), low),
        pltpu.VMEM((outer, chunks, block, HD), low),
        pltpu.VMEM((vis, batch * text, width), low),
        pltpu.VMEM((heads, share, cols), full),
        pltpu.VMEM((heads, share, cols), low),
        pltpu.VMEM((heads, share, cols), low),
        dma((batch, outer, 2)), dma((batch, outer, 2)), dma((batch, outer, 6)), dma((batch, outer, 6)),
        dma((inner,)), dma((inner,)), dma((outer,)), dma((outer,)), dma((inner,)), dma((inner,)),
        dma((inner, chunks)), dma((inner, chunks)), dma((outer,)), dma((outer,)),
        dma((outer, 2)), dma((outer, 2)), dma((outer, 6)), dma((outer, 6)),
        dma((heads,)), dma((heads,)),
    ]
    results = pl.pallas_call(
        functools.partial(kernel, outer, inner, heads),
        out_shape=(
            jax.ShapeDtypeStruct((batch, vis * text // heads, cols), low),
            jax.ShapeDtypeStruct(keys.shape, low),
            jax.ShapeDtypeStruct(values.shape, low),
        ),
        in_specs=[pl.BlockSpec(memory_space=pltpu.HBM)] * 5,
        out_specs=(pl.BlockSpec(memory_space=pltpu.VMEM),) + (pl.BlockSpec(memory_space=pltpu.HBM),) * 2,
        scratch_shapes=scratch,
        compiler_params=pltpu.CompilerParams(
            collective_id=0, has_side_effects=True, vmem_limit_bytes=60 * 1024 * 1024
        ),
    )(queries, d_out, keys, values, q_weight)
    return pl.pallas_call(
        leave,
        out_shape=tuple(jax.ShapeDtypeStruct(x.shape, x.dtype) for x in results),
        in_specs=[pl.BlockSpec(memory_space=pltpu.VMEM)] * len(results),
        out_specs=(pl.BlockSpec(memory_space=pltpu.HBM),) * len(results),
        scratch_shapes=[dma((len(results),))],
    )(*results)


def solution(mesh):
    placed = (
        P(None, "vis", "head"),
        P(None, "vis", "head"),
        P(None, "vis", "head"),
        P(None, "vis", "head"),
        P("vis", "head"),
    )
    return jax.shard_map(
        functools.partial(per_device, mesh.shape["vis"], mesh.shape["head"]),
        mesh=mesh,
        in_specs=placed,
        out_specs=(P(None, "head", "vis"), P(None, "vis", "head"), P(None, "vis", "head")),
        check_vma=False,
    )
```
